512 devices in a mesh: row: 16 (over y, x), col: 32 (over z, core).
Axes of the slice: x: 4, y: 4, z: 16, core: 2. Of those that a mesh axis runs over, the one named last changes fastest.
Arguments:
- matrix: float32 [16, 8, 128, 32, 4, 128], P('row', None, None, 'col'), as said below
Outputs:
- factored: float32 [16, 8, 128, 32, 4, 128], P('row', None, None, 'col')
Inputs may be any that keep to these rules, and one draw needn't show every extreme that they name: matrix is a Gaussian-process covariance matrix with a nugget term: symmetric and positive definite.
All inputs are finite; a program needn't handle non-finite values.
Results may differ from the reference program's by a relative error of at most 0.0003.
Values sent between devices are 32-bit elements; how exact they have to be, the bound alone decides.
No kernel may reach another device: no remote copies, remote signals or barrier semaphores. Data moves between devices by JAX's collectives and lax.ppermute only.
A program may use at most 64 MiB of HBM per device.

```python
import jax
import jax.numpy as jnp
from jax import lax

N = 16384
NB = 128
STEPS = 2
RB = 8
CB = 4


def draw_matrix(key, part):
    key = jax.random.fold_in(key, 11)
    point_key, scale_key = jax.random.split(key, 2)
    nugget = 0.5
    points = jax.random.uniform(point_key, (4, N), jnp.float32, 0.0, 1.0)
    amplitude = jnp.exp(jax.random.uniform(scale_key, (N,), jnp.float32, -0.35, 0.35))
    length_scale = 0.5
    squared = jnp.zeros((N, N), jnp.float32)
    for coordinate in range(4):
        difference = points[coordinate][:, None] - points[coordinate][None, :]
        squared = squared + difference * difference
    ident = jnp.arange(N)[:, None] == jnp.arange(N)[None, :]
    distance = jnp.sqrt(jnp.where(ident, 1.0, squared))
    kernel = jnp.where(ident, 1.0 + nugget, jnp.exp(-distance / length_scale))
    full = kernel * amplitude[:, None] * amplitude[None, :]
    nrow = N // (NB * RB)
    ncol = N // (NB * CB)
    return full.reshape(RB, nrow, NB, CB, ncol, NB).transpose(1, 0, 2, 4, 3, 5)


def setup_inputs(seed: int = 0) -> dict:
    seeds = jax.random.split(jax.random.key(seed), 2)
    return {
        "matrix": draw_matrix(jax.random.fold_in(seeds[1], 71), 0),
    }


def reference(matrix):
    nrow, rblk, width, ncol, cblk, _ = matrix.shape
    order = nrow * rblk * width
    store = matrix.transpose(1, 0, 2, 4, 3, 5).reshape(order, order)
    for step in range(STEPS):
        start = step * NB
        finish = start + NB
        factor = jnp.linalg.cholesky(store[start:finish, start:finish])
        inverse = lax.linalg.triangular_solve(factor, jnp.eye(NB, dtype=jnp.float32), left_side=True, lower=True)
        panel = jnp.dot(store[finish:, start:finish], inverse.T, precision=lax.Precision.HIGHEST)
        store = store.at[start:finish, start:finish].set(factor)
        store = store.at[finish:, start:finish].set(panel)
        store = store.at[finish:, finish:].add(-jnp.dot(panel, panel.T, precision=lax.Precision.HIGHEST))
    store = jnp.tril(store)
    return store.reshape(rblk, nrow, width, cblk, ncol, width).transpose(1, 0, 2, 4, 3, 5)
```

```python
import jax
import jax.numpy as jnp
from jax import lax
from jax.experimental import pallas as pl
from jax.experimental.pallas import tpu as pltpu
from jax.sharding import PartitionSpec as P

HIGHEST = lax.Precision.HIGHEST
ROWS = 16
COLS = 32
LAYERS = 16
NB = 128
HALF = 64
PIECE = 8
STEP_ROWS = 256


def mm(a, b):
    return lax.dot_general(
        a, b, (((1,), (0,)), ((), ())), precision=HIGHEST, preferred_element_type=jnp.float32
    )


def mmt(a, b):
    return lax.dot_general(
        a, b, (((1,), (1,)), ((), ())), precision=HIGHEST, preferred_element_type=jnp.float32
    )


def eliminate(block, work):
    n = HALF
    shape = (8, 2 * n)
    lane = lax.broadcasted_iota(jnp.int32, shape, 1)
    sub = lax.broadcasted_iota(jnp.int32, shape, 0)
    work[:, :n] = block
    parts = []
    for i in range(n // 8):
        unit = jnp.where(lane == n + 8 * i + sub, 1.0, 0.0)
        parts.append(jnp.where(lane < n, work[8 * i : 8 * i + 8, :], unit))
    out = []
    for a in range(n // 8):
        rest = range(a + 1, n // 8)
        cols = []
        for j in range(8):
            k = 8 * a + j
            cols.append(
                {i: jnp.broadcast_to(parts[i][:, k : k + 1], shape) for i in range(a, n // 8)}
            )
        e = [
            [jnp.broadcast_to(cols[j][a][i : i + 1, :], shape) for j in range(i + 1)]
            for i in range(8)
        ]
        rows = [jnp.broadcast_to(parts[a][k : k + 1, :], shape) for k in range(8)]
        strip = None
        for k in range(8):
            inv = 1.0 / e[k][k]
            for i in range(k + 1, 8):
                low = e[i][k] * inv
                for j in range(k + 1, i + 1):
                    e[i][j] = e[i][j] - low * e[j][k]
                rows[i] = rows[i] - low * rows[k]
            root = lax.rsqrt(e[k][k])
            root = root * (1.5 - 0.5 * e[k][k] * root * root)
            done = rows[k] * root
            strip = done if k == 0 else jnp.where(sub == k, done, strip)
            for i in rest:
                m = cols[k][i] * inv
                for j in range(k + 1, 8):
                    cols[j][i] = cols[j][i] - m * e[j][k]
                parts[i] = parts[i] - m * rows[k]
        out.append(strip)
    full = jnp.concatenate(out, axis=0)
    r = lax.broadcasted_iota(jnp.int32, (n, n), 0)
    c = lax.broadcasted_iota(jnp.int32, (n, n), 1)
    return jnp.where(r <= c, full[:, :n], 0.0), jnp.where(r >= c, full[:, n:], 0.0)


def factor_block(s, work, upper):
    h = HALF
    u11, i11 = eliminate(s[:h, :h], work)
    l21 = mmt(s[h:, :h], i11)
    t21 = mm(l21, i11)
    u22, i22 = eliminate(s[h:, h:] - mmt(l21, l21), work)
    upper[:h, :h] = u11
    upper[:h, h:] = l21.T
    upper[h:, :h] = jnp.zeros((h, h), jnp.float32)
    upper[h:, h:] = u22
    return i11, -mm(i22, t21), i22


def factor_kernel(place, own, other, inv, l11, l21, l22, work, upper):
    h, n = HALF, NB
    even = place[1] % 2 == 0

    def block(side, half):
        a, b = own[:, half].reshape(n, n), other[:, half].reshape(n, n)
        return jnp.where(even, a, b) if side == 0 else jnp.where(even, b, a)

    def put(o, blocks):
        inv[o : o + h, o : o + h] = blocks[0]
        inv[o : o + h, o + h : o + n] = jnp.zeros((h, h), jnp.float32)
        inv[o + h : o + n, o : o + h] = blocks[1]
        inv[o + h : o + n, o + h : o + n] = blocks[2]

    put(0, factor_block(block(0, 0), work, upper))
    l11[...] = upper[...].T
    i11 = inv[:n, :n]
    p = mmt(block(0, 1), i11)
    t = mm(p, i11)
    l21[...] = p
    put(n, factor_block(block(1, 1) - mmt(p, p), work, upper))
    l22[...] = upper[...].T
    inv[:n, n:] = jnp.zeros((n, n), jnp.float32)
    inv[n:, :n] = -mm(inv[n:, n:], t)


def factorise(place, own, other):
    block = jax.ShapeDtypeStruct((NB, NB), jnp.float32)
    whole = jax.ShapeDtypeStruct((2 * NB, 2 * NB), jnp.float32)
    vmem = pl.BlockSpec(memory_space=pltpu.VMEM)
    return pl.pallas_call(
        factor_kernel,
        in_specs=[pl.BlockSpec(memory_space=pltpu.SMEM), vmem, vmem],
        out_specs=[vmem] * 4,
        out_shape=[whole, block, block, block],
        scratch_shapes=[pltpu.VMEM((HALF, NB), jnp.float32), pltpu.VMEM((NB, NB), jnp.float32)],
        name="factorise",
    )(place, own, other)


def update_kernel(place, inv, l11, l21, l22, own, other, strips, store, out, mirrored):
    n = NB
    step = pl.program_id(0)
    row, col = place[0], place[1]
    even = col % 2 == 0

    @pl.when(step == 0)
    def _():
        top = [[] for _ in range(4)]
        for half in range(2):
            for j in range(4):
                for p in range(ROWS):
                    top[j].append(strips[p, half, pl.ds(j, PIECE, stride=4), :])
        whole = jnp.concatenate([jnp.concatenate(t, axis=0) for t in top], axis=1)
        mirrored[...] = mm(inv[...], whole)

    a, b = own[...], other[...]
    left, right = jnp.where(even, a, b), jnp.where(even, b, a)
    panel = mmt(jnp.concatenate([left, right], axis=1), inv[...])
    update = mm(panel, mirrored[...])
    local = lax.broadcasted_iota(jnp.int32, (STEP_ROWS, n), 0)
    grow = (step * (STEP_ROWS // n) + local // n) * ROWS + row
    rid = grow * n + local % n
    lane = lax.broadcasted_iota(jnp.int32, (STEP_ROWS, n), 1)
    for j in range(4):
        cid = (j * COLS + col) * n + lane
        rows = pl.ds(j, STEP_ROWS, stride=4)
        out[rows, :] = jnp.where(rid >= cid, store[rows, :] - update[:, j * n : (j + 1) * n], 0.0)

    @pl.when(col < 2)
    def _():
        first = jnp.where(col == 0, l11[...], 0.0)
        second = jnp.where(col == 0, l21[...], l22[...])
        pad = jnp.zeros((STEP_ROWS - n, n), jnp.float32)
        solved = jnp.where(col == 0, panel[:, :n], panel[:, n:])
        solved = jnp.where(grow == 0, jnp.concatenate([first, pad], axis=0), solved)
        solved = jnp.where(grow == 1, jnp.concatenate([second, pad], axis=0), solved)
        out[pl.ds(0, STEP_ROWS, stride=4), :] = jnp.where(rid >= col * n + lane, solved, 0.0)


def update(place, inv, l11, l21, l22, own, other, strips, view):
    fixed = pl.BlockSpec(memory_space=pltpu.VMEM)
    rows = pl.BlockSpec((STEP_ROWS, NB), lambda i: (i, 0))
    wide = pl.BlockSpec((4 * STEP_ROWS, NB), lambda i: (i, 0))
    return pl.pallas_call(
        update_kernel,
        grid=(view.shape[0] // (4 * STEP_ROWS),),
        in_specs=[pl.BlockSpec(memory_space=pltpu.SMEM)] + [fixed] * 4 + [rows, rows, fixed, wide],
        out_specs=wide,
        out_shape=jax.ShapeDtypeStruct(view.shape, jnp.float32),
        scratch_shapes=[pltpu.VMEM((2 * NB, 4 * NB), jnp.float32)],
        name="update",
    )(place, inv, l11, l21, l22, own, other, strips, view)


def z_pairs(held, stride):
    pairs = []
    for z in held:
        pairs.append((2 * z, 2 * ((z + stride) % LAYERS)))
        pairs.append((2 * z + 1, 2 * ((z - stride) % LAYERS) + 1))
    return pairs


def swap_core(value):
    return lax.ppermute(value, "col", [(c, c ^ 1) for c in range(COLS)])


def shards(matrix):
    row = lax.axis_index("row")
    col = lax.axis_index("col")
    place = jnp.stack([row, col])
    layer = jnp.where(col % 2 == 0, col // 2, (LAYERS - col // 2) % LAYERS)
    view = matrix.reshape(-1, NB)
    column = view.reshape(-1, 4, NB)[:, 0, :]

    def spread(value, stride, after=None):
        held = list(range(0, LAYERS, 2 * stride))
        moved = lax.ppermute(value, "col", z_pairs(held, stride))
        if after is not None:
            value, moved, _ = lax.optimization_barrier((value, moved, after))
        return jnp.where(layer % (2 * stride) == stride, moved, value)

    pieces = view[: 4 * NB].reshape(ROWS, 4 * PIECE, NB)
    pieces = lax.all_to_all(pieces, "row", 0, 0, tiled=True)
    column = spread(column, 8, pieces)
    pieces = jnp.broadcast_to(pieces[:2][None], (ROWS, 2, 4 * PIECE, NB))
    pieces, column = lax.optimization_barrier((pieces, column))
    strips = lax.all_to_all(pieces, "row", 0, 0, tiled=True)
    column = spread(column, 4, strips)

    corner = strips[:, :, ::4, :]
    corner, column = lax.optimization_barrier((corner, column))
    for held, stride in (([0], 4), ([0, 4, 8, 12], 1)):
        parts = {q: lax.ppermute(corner, "col", z_pairs(held, q * stride)) for q in (2, 1, 3)}
        part = (layer // stride) % 4
        kept = jnp.where(part == 2, parts[2], corner)
        corner = jnp.where(part == 1, parts[1], jnp.where(part == 3, parts[3], kept))
        if stride == 4:
            column = spread(column, 2, corner)
            corner, column = lax.optimization_barrier((corner, column))
    corner_other = swap_core(corner)
    column = spread(column, 1, corner_other)
    corner, corner_other, column = lax.optimization_barrier((corner, corner_other, column))
    column_other = swap_core(column)
    inv, l11, l21, l22 = factorise(place, corner, corner_other)
    out = update(place, inv, l11, l21, l22, column, column_other, strips, view)
    return out.reshape(matrix.shape)


def solution(mesh):
    spec = P("row", None, None, "col", None, None)
    return jax.shard_map(shards, mesh=mesh, in_specs=(spec,), out_specs=spec, check_vma=False)
```

```python
import jax
import jax.numpy as jnp
from jax import lax
from jax.experimental import pallas as pl
from jax.experimental.pallas import tpu as pltpu
from jax.sharding import PartitionSpec as P

HIGHEST = lax.Precision.HIGHEST
ROWS = 16
COLS = 32
LAYERS = 16
SIDE = 4
NB = 128
HALF = 64
PIECE = 8
CHUNKS = 2


def mm(a, b):
    return lax.dot_general(
        a, b, (((1,), (0,)), ((), ())), precision=HIGHEST, preferred_element_type=jnp.float32
    )


def mmt(a, b):
    return lax.dot_general(
        a, b, (((1,), (1,)), ((), ())), precision=HIGHEST, preferred_element_type=jnp.float32
    )


def split(a):
    high = a.astype(jnp.bfloat16)
    return high, (a - high.astype(jnp.float32)).astype(jnp.bfloat16)


def mm3(a, b):
    ah, al = split(a)
    bh, bl = b
    dot = lambda x, y: lax.dot_general(x, y, (((1,), (0,)), ((), ())), preferred_element_type=jnp.float32)
    return dot(ah, bh) + (dot(ah, bl) + dot(al, bh))


def eliminate(block, work):
    n = HALF
    shape = (8, 2 * n)
    lane = lax.broadcasted_iota(jnp.int32, shape, 1)
    sub = lax.broadcasted_iota(jnp.int32, shape, 0)
    work[:, :n] = block
    parts = []
    for i in range(n // 8):
        unit = jnp.where(lane == n + 8 * i + sub, 1.0, 0.0)
        parts.append(jnp.where(lane < n, work[8 * i : 8 * i + 8, :], unit))
    out = []
    for a in range(n // 8):
        rest = range(a + 1, n // 8)
        cols = []
        for j in range(8):
            k = 8 * a + j
            cols.append(
                {i: jnp.broadcast_to(parts[i][:, k : k + 1], shape) for i in range(a, n // 8)}
            )
        e = [
            [jnp.broadcast_to(cols[j][a][i : i + 1, :], shape) for j in range(i + 1)]
            for i in range(8)
        ]
        rows = [jnp.broadcast_to(parts[a][k : k + 1, :], shape) for k in range(8)]
        strip = None
        for k in range(8):
            inv = 1.0 / e[k][k]
            for i in range(k + 1, 8):
                low = e[i][k] * inv
                for j in range(k + 1, i + 1):
                    e[i][j] = e[i][j] - low * e[j][k]
                rows[i] = rows[i] - low * rows[k]
            root = lax.rsqrt(e[k][k])
            root = root * (1.5 - 0.5 * e[k][k] * root * root)
            done = rows[k] * root
            strip = done if k == 0 else jnp.where(sub == k, done, strip)
            for i in rest:
                m = cols[k][i] * inv
                for j in range(k + 1, 8):
                    cols[j][i] = cols[j][i] - m * e[j][k]
                parts[i] = parts[i] - m * rows[k]
        out.append(strip)
    full = jnp.concatenate(out, axis=0)
    r = lax.broadcasted_iota(jnp.int32, (n, n), 0)
    c = lax.broadcasted_iota(jnp.int32, (n, n), 1)
    return jnp.where(r <= c, full[:, :n], 0.0), jnp.where(r >= c, full[:, n:], 0.0)


def factor_block(s, work, upper):
    h = HALF
    u11, i11 = eliminate(s[:h, :h], work)
    l21 = mmt(s[h:, :h], i11)
    t21 = mm(l21, i11)
    u22, i22 = eliminate(s[h:, h:] - mmt(l21, l21), work)
    upper[:h, :h] = u11
    upper[:h, h:] = l21.T
    upper[h:, :h] = jnp.zeros((h, h), jnp.float32)
    upper[h:, h:] = u22
    return i11, -mm(i22, t21), i22


def factor_kernel(col, own, other, packed, l11, l21, l22, work, upper, inv):
    h, n = HALF, NB
    even = col[0] == 0

    def block(side, half):
        a, b = own[half], other[half]
        return jnp.where(even, a, b) if side == 0 else jnp.where(even, b, a)

    def put(to, blocks):
        to[:h, :h] = blocks[0]
        to[:h, h:] = jnp.zeros((h, h), jnp.float32)
        to[h:, :h] = blocks[1]
        to[h:, h:] = blocks[2]

    @pl.when(col[0] < 2)
    def _():
        put(inv.at[0], factor_block(block(0, 0), work, upper))
        l11[...] = upper[...].T
        i11 = inv[0]
        p = mmt(block(0, 1), i11)
        t = mm(p, i11)
        l21[...] = p
        put(inv.at[1], factor_block(block(1, 1) - mmt(p, p), work, upper))
        l22[...] = upper[...].T
        i22 = inv[1]
        r = lax.broadcasted_iota(jnp.int32, (n, n), 0)
        c = lax.broadcasted_iota(jnp.int32, (n, n), 1)
        packed[:n] = jnp.where(r >= c, i11, i22.T)
        packed[n : 2 * n] = -mm(i22, t)
        diagonal = jnp.sum(jnp.where(r == c, i22, 0.0), axis=0, keepdims=True)
        packed[2 * n :] = jnp.broadcast_to(diagonal, (8, n))


def factorise(col, own, other):
    block = jax.ShapeDtypeStruct((NB, NB), jnp.float32)
    vmem = pl.BlockSpec(memory_space=pltpu.VMEM)
    return pl.pallas_call(
        factor_kernel,
        in_specs=[pl.BlockSpec(memory_space=pltpu.SMEM), vmem, vmem],
        out_specs=[vmem] * 4,
        out_shape=[jax.ShapeDtypeStruct((2 * NB + 8, NB), jnp.float32), block, block, block],
        scratch_shapes=[
            pltpu.VMEM((HALF, NB), jnp.float32),
            pltpu.VMEM((NB, NB), jnp.float32),
            pltpu.VMEM((2, NB, NB), jnp.float32),
        ],
        name="factorise",
    )(col, own, other)


def is_top(row):
    x = row % SIDE
    return (x == 0) | (x == SIDE - 1)


def update_kernel(at_row, at_col, held, two, one, three, l11, l21, l22, own, other, here, there, store, out, data, sems, outs):
    n = NB
    chunks = data.shape[0]
    rows_of = data.shape[1]
    loads = [pltpu.make_async_copy(store.at[pl.ds(i * rows_of, rows_of)], data.at[i], sems.at[i]) for i in range(chunks)]
    saves = [pltpu.make_async_copy(data.at[i], out.at[pl.ds(i * rows_of, rows_of)], outs.at[i]) for i in range(chunks)]
    for load in loads:
        load.start()
    row, col = at_row[0], at_col[0]
    even = col % 2 == 0
    top = is_top(row)
    halves = [[], []]
    for j in range(4):
        a = here[pl.ds(j, n, stride=4), :]
        b = there[pl.ds(j, n, stride=4), :]
        halves[0].append(jnp.where(top, a, b))
        halves[1].append(jnp.where(top, b, a))
    whole = jnp.concatenate([jnp.concatenate(h, axis=1) for h in halves], axis=0)
    r = lax.broadcasted_iota(jnp.int32, (n, n), 0)
    c = lax.broadcasted_iota(jnp.int32, (n, n), 1)
    core, z = col % 2, col // 2
    step = jnp.where(core == 0, z, LAYERS - z) % 4
    packed = jnp.where(step == 2, two[...], held[...])
    packed = jnp.where(step == 1, one[...], jnp.where(step == 3, three[...], packed))
    shared = packed[:n]
    i11 = jnp.where(r >= c, shared, 0.0)
    diagonal = jnp.where(r == c, packed[2 * n : 2 * n + 1], 0.0)
    i22 = jnp.where(r > c, shared.T, diagonal)
    inverse = jnp.concatenate(
        [
            jnp.concatenate([i11, jnp.zeros((n, n), jnp.float32)], axis=1),
            jnp.concatenate([packed[n : 2 * n], i22], axis=1),
        ],
        axis=0,
    )
    mirrored = split(mm(inverse, whole))
    count = rows_of // 4
    local = lax.broadcasted_iota(jnp.int32, (count, n), 0)
    lane = lax.broadcasted_iota(jnp.int32, (count, n), 1)
    for i in range(chunks):
        span = pl.ds(i * count, count)
        a, b = own[span, :], other[span, :]
        left, right = jnp.where(even, a, b), jnp.where(even, b, a)
        panel = mmt(jnp.concatenate([left, right], axis=1), inverse)
        update = mm3(panel, mirrored)
        grow = (i * (count // n) + local // n) * ROWS + row
        rid = grow * n + local % n
        loads[i].wait()
        for j in range(4):
            cid = (j * COLS + col) * n + lane
            rows = pl.ds(j, count, stride=4)
            kept = data[i, rows, :] - update[:, j * n : (j + 1) * n]
            data[i, rows, :] = jnp.where(rid >= cid, kept, 0.0)

        @pl.when(col < 2)
        def _():
            solved = jnp.where(col == 0, panel[:, :n], panel[:, n:])
            if i == 0:
                first = jnp.where(col == 0, l11[...], 0.0)
                second = jnp.where(col == 0, l21[...], l22[...])
                solved = jnp.where(grow == 0, jnp.tile(first, (count // n, 1)), solved)
                solved = jnp.where(grow == 1, jnp.tile(second, (count // n, 1)), solved)
            data[i, pl.ds(0, count, stride=4), :] = jnp.where(rid >= col * n + lane, solved, 0.0)

        saves[i].start()
    for save in saves:
        save.wait()


def update(row, col, inverse, l11, l21, l22, own, other, here, there, view):
    vmem = pl.BlockSpec(memory_space=pltpu.VMEM)
    smem = pl.BlockSpec(memory_space=pltpu.SMEM)
    anywhere = pl.BlockSpec(memory_space=pl.ANY)
    return pl.pallas_call(
        update_kernel,
        in_specs=[smem] * 2 + [vmem] * 11 + [anywhere],
        out_specs=anywhere,
        out_shape=jax.ShapeDtypeStruct(view.shape, jnp.float32),
        scratch_shapes=[
            pltpu.VMEM((CHUNKS, view.shape[0] // CHUNKS, NB), jnp.float32),
            pltpu.SemaphoreType.DMA((CHUNKS,)),
            pltpu.SemaphoreType.DMA((CHUNKS,)),
        ],
        name="update",
    )(row, col, *inverse, l11, l21, l22, own, other, here, there, view)


def z_pairs(root, held, stride):
    pairs = []
    for layer in held:
        for core, sign in ((0, 1), (1, -1)):
            a = (root + sign * layer) % LAYERS
            b = (root + sign * (layer + stride)) % LAYERS
            if root == 0 or b > 0:
                pairs.append((2 * a + core, 2 * b + core))
    return pairs


def plane_pairs(first, second):
    pairs = []
    for core, rows in ((0, first), (1, second)):
        for z in range(LAYERS):
            pairs += [(a * COLS + 2 * z + core, b * COLS + 2 * z + core) for a, b in rows]
    return pairs


def shards(matrix):
    row = lax.axis_index("row")
    col = lax.axis_index("col")
    at_row, at_col = row.reshape(1), col.reshape(1)
    core, z = col % 2, col // 2
    layer = jnp.where(core == 0, z, (LAYERS - z) % LAYERS)
    after = jnp.where(core == 0, (z + LAYERS - 1) % LAYERS, (LAYERS + 1 - z) % LAYERS)
    x, y = row % SIDE, row // SIDE
    view = matrix.reshape(-1, NB)

    def tie(*values):
        return lax.optimization_barrier(values)

    def send(value, pairs):
        return lax.ppermute(value, "col", pairs)

    def send_plane(value, first, second):
        return lax.ppermute(value, ("row", "col"), plane_pairs(first, second))

    def choose(step, held, parts):
        kept = jnp.where(step == 2, parts[0], held)
        return jnp.where(step == 1, parts[1], jnp.where(step == 3, parts[2], kept))

    across = lambda ys: [(SIDE * q + a, SIDE * q + b) for q in ys for a, b in ((0, 3), (1, 2))]
    along = lambda ys, by, xs: [(SIDE * q + i, SIDE * (q + by) + i) for q in ys for i in xs]
    strip, view = tie(view[: 4 * NB], view)
    moved = send_plane(strip, across([0]), along([0], 2, (0, 1)))
    column = view.reshape(-1, 4, NB)[:, 0, :]
    sent = send(column, [(0, 2), (1, 3)])
    strip = jnp.where(jnp.where(core == 0, x >= 2, y == 2), moved, strip)
    moved = send_plane(strip, along([0], 2, range(4)), along([0, 2], 1, (0, 1)))
    strip = jnp.where(jnp.where(core == 0, y == 2, y % 2 == 1), moved, strip)
    moved = send_plane(strip, along([0, 2], 1, range(4)), across(range(4)))
    _, sent, column = tie(strip, sent, column)
    column = jnp.where(z == 1, sent, column)
    sent = send(column, z_pairs(1, [0], 4))
    strip = jnp.where(jnp.where(core == 0, y % 2 == 1, x >= 2), moved, strip)
    swap = [(i, i ^ 1) for i in range(ROWS)]
    mine = strip[::4]
    theirs = send_plane(mine, swap, swap)
    _, sent, column = tie(strip, sent, column)
    column = jnp.where((z != 0) & (after == 4), sent, column)
    sent = send(column, z_pairs(1, [0], 12) + z_pairs(1, [4], 4))
    column = jnp.where((z != 0) & ((after == 8) | (after == 12)), sent, column)
    sent = send(column, z_pairs(1, range(0, 16, 4), 2))

    strip, theirs = tie(strip, theirs)
    facing = send_plane(strip, swap, swap)
    top = is_top(row)
    corner = jnp.stack([jnp.where(top, mine, theirs), jnp.where(top, theirs, mine)])
    other = send(corner, [(0, 1), (1, 0)])
    _, sent, column = tie(other, sent, column)
    column = jnp.where((z != 0) & (after % 4 == 2), sent, column)
    sent = send(column, z_pairs(1, range(0, 16, 2), 1))
    corner, other, column = tie(corner, other, column)
    inv, l11, l21, l22 = factorise(at_col, corner, other)
    inv, facing = tie(inv, facing)

    parts = [send(inv, z_pairs(0, [0], 4 * q)) for q in (2, 1, 3)]
    *parts, column = tie(*parts, column)
    inv = choose(layer // 4, inv, parts)
    _, sent, column = tie(inv, sent, column)
    parts = [send(inv, z_pairs(0, [0, 4, 8, 12], q)) for q in (2, 1, 3)]
    parts[0], sent, column = tie(parts[0], sent, column)
    column = jnp.where((z != 0) & (after % 2 == 1), sent, column)
    column_other = send(column, [(c, c ^ 1) for c in range(COLS)])
    *parts, column = tie(*parts, column)
    out = update(at_row, at_col, [inv, *parts], l11, l21, l22, column, column_other, strip, facing, view)
    return out.reshape(matrix.shape)


def solution(mesh):
    spec = P("row", None, None, "col", None, None)
    return jax.shard_map(shards, mesh=mesh, in_specs=(spec,), out_specs=spec, check_vma=False)
```

```python
import jax
import jax.numpy as jnp
from jax import lax
from jax.experimental import pallas as pl
from jax.experimental.pallas import tpu as pltpu
from jax.sharding import PartitionSpec as P

HIGHEST = lax.Precision.HIGHEST
ROWS = 16
COLS = 32
LAYERS = 16
SIDE = 4
NB = 128
HALF = 64
PIECE = 8
CHUNKS = 2


def mm(a, b):
    return lax.dot_general(
        a, b, (((1,), (0,)), ((), ())), precision=HIGHEST, preferred_element_type=jnp.float32
    )


def mmt(a, b):
    return lax.dot_general(
        a, b, (((1,), (1,)), ((), ())), precision=HIGHEST, preferred_element_type=jnp.float32
    )


def split(a):
    high = a.astype(jnp.bfloat16)
    return high, (a - high.astype(jnp.float32)).astype(jnp.bfloat16)


def mm3(a, b):
    ah, al = split(a)
    bh, bl = b
    dot = lambda x, y: lax.dot_general(x, y, (((1,), (0,)), ((), ())), preferred_element_type=jnp.float32)
    return dot(ah, bh) + (dot(ah, bl) + dot(al, bh))


def eliminate(block, work):
    n = HALF
    shape = (8, 2 * n)
    lane = lax.broadcasted_iota(jnp.int32, shape, 1)
    sub = lax.broadcasted_iota(jnp.int32, shape, 0)
    work[:, :n] = block
    parts = []
    for i in range(n // 8):
        unit = jnp.where(lane == n + 8 * i + sub, 1.0, 0.0)
        parts.append(jnp.where(lane < n, work[8 * i : 8 * i + 8, :], unit))
    out = []
    for a in range(n // 8):
        rest = range(a + 1, n // 8)
        cols = []
        for j in range(8):
            k = 8 * a + j
            cols.append(
                {i: jnp.broadcast_to(parts[i][:, k : k + 1], shape) for i in range(a, n // 8)}
            )
        e = [
            [jnp.broadcast_to(cols[j][a][i : i + 1, :], shape) for j in range(i + 1)]
            for i in range(8)
        ]
        rows = [jnp.broadcast_to(parts[a][k : k + 1, :], shape) for k in range(8)]
        strip = None
        for k in range(8):
            inv = 1.0 / e[k][k]
            for i in range(k + 1, 8):
                low = e[i][k] * inv
                for j in range(k + 1, i + 1):
                    e[i][j] = e[i][j] - low * e[j][k]
                rows[i] = rows[i] - low * rows[k]
            root = lax.rsqrt(e[k][k])
            root = root * (1.5 - 0.5 * e[k][k] * root * root)
            done = rows[k] * root
            strip = done if k == 0 else jnp.where(sub == k, done, strip)
            for i in rest:
                m = cols[k][i] * inv
                for j in range(k + 1, 8):
                    cols[j][i] = cols[j][i] - m * e[j][k]
                parts[i] = parts[i] - m * rows[k]
        out.append(strip)
    full = jnp.concatenate(out, axis=0)
    r = lax.broadcasted_iota(jnp.int32, (n, n), 0)
    c = lax.broadcasted_iota(jnp.int32, (n, n), 1)
    return jnp.where(r <= c, full[:, :n], 0.0), jnp.where(r >= c, full[:, n:], 0.0)


def factor_block(s, work, upper):
    h = HALF
    u11, i11 = eliminate(s[:h, :h], work)
    l21 = mmt(s[h:, :h], i11)
    t21 = mm(l21, i11)
    u22, i22 = eliminate(s[h:, h:] - mmt(l21, l21), work)
    upper[:h, :h] = u11
    upper[:h, h:] = l21.T
    upper[h:, :h] = jnp.zeros((h, h), jnp.float32)
    upper[h:, h:] = u22
    return i11, -mm(i22, t21), i22


def factor_kernel(col, own, other, packed, l11, l21, l22, work, upper, inv):
    h, n = HALF, NB
    even = col[0] == 0

    def block(side, half):
        a, b = own[half], other[half]
        return jnp.where(even, a, b) if side == 0 else jnp.where(even, b, a)

    def put(to, blocks):
        to[:h, :h] = blocks[0]
        to[:h, h:] = jnp.zeros((h, h), jnp.float32)
        to[h:, :h] = blocks[1]
        to[h:, h:] = blocks[2]

    @pl.when(col[0] < 2)
    def _():
        put(inv.at[0], factor_block(block(0, 0), work, upper))
        l11[...] = upper[...].T
        i11 = inv[0]
        p = mmt(block(0, 1), i11)
        t = mm(p, i11)
        l21[...] = p
        put(inv.at[1], factor_block(block(1, 1) - mmt(p, p), work, upper))
        l22[...] = upper[...].T
        i22 = inv[1]
        r = lax.broadcasted_iota(jnp.int32, (n, n), 0)
        c = lax.broadcasted_iota(jnp.int32, (n, n), 1)
        packed[:n] = jnp.where(r >= c, i11, i22.T)
        packed[n : 2 * n] = -mm(i22, t)
        diagonal = jnp.sum(jnp.where(r == c, i22, 0.0), axis=0, keepdims=True)
        packed[2 * n :] = jnp.broadcast_to(diagonal, (8, n))


def factorise(col, own, other):
    block = jax.ShapeDtypeStruct((NB, NB), jnp.float32)
    vmem = pl.BlockSpec(memory_space=pltpu.VMEM)
    return pl.pallas_call(
        factor_kernel,
        in_specs=[pl.BlockSpec(memory_space=pltpu.SMEM), vmem, vmem],
        out_specs=[vmem] * 4,
        out_shape=[jax.ShapeDtypeStruct((2 * NB + 8, NB), jnp.float32), block, block, block],
        scratch_shapes=[
            pltpu.VMEM((HALF, NB), jnp.float32),
            pltpu.VMEM((NB, NB), jnp.float32),
            pltpu.VMEM((2, NB, NB), jnp.float32),
        ],
        name="factorise",
    )(col, own, other)


def is_top(row):
    x = row % SIDE
    return (x == 0) | (x == SIDE - 1)


def update_kernel(at_row, at_col, held, two, one, three, l11, l21, l22, own, other, here, there, store, out, data, sems, outs):
    n = NB
    chunks = data.shape[0]
    rows_of = data.shape[1]
    loads = [pltpu.make_async_copy(store.at[pl.ds(i * rows_of, rows_of)], data.at[i], sems.at[i]) for i in range(chunks)]
    saves = [pltpu.make_async_copy(data.at[i], out.at[pl.ds(i * rows_of, rows_of)], outs.at[i]) for i in range(chunks)]
    for load in loads:
        load.start()
    row, col = at_row[0], at_col[0]
    even = col % 2 == 0
    top = is_top(row)
    halves = [[], []]
    for j in range(4):
        a = here[pl.ds(j, n, stride=4), :]
        b = there[pl.ds(j, n, stride=4), :]
        halves[0].append(jnp.where(top, a, b))
        halves[1].append(jnp.where(top, b, a))
    whole = jnp.concatenate([jnp.concatenate(h, axis=1) for h in halves], axis=0)
    r = lax.broadcasted_iota(jnp.int32, (n, n), 0)
    c = lax.broadcasted_iota(jnp.int32, (n, n), 1)
    core, z = col % 2, col // 2
    step = jnp.where(core == 0, z, LAYERS - z) % 4
    packed = jnp.where(step == 2, two[...], held[...])
    packed = jnp.where(step == 1, one[...], jnp.where(step == 3, three[...], packed))
    shared = packed[:n]
    i11 = jnp.where(r >= c, shared, 0.0)
    diagonal = jnp.where(r == c, packed[2 * n : 2 * n + 1], 0.0)
    i22 = jnp.where(r > c, shared.T, diagonal)
    inverse = jnp.concatenate(
        [
            jnp.concatenate([i11, jnp.zeros((n, n), jnp.float32)], axis=1),
            jnp.concatenate([packed[n : 2 * n], i22], axis=1),
        ],
        axis=0,
    )
    mirrored = split(mm(inverse, whole))
    count = rows_of // 4
    local = lax.broadcasted_iota(jnp.int32, (count, n), 0)
    lane = lax.broadcasted_iota(jnp.int32, (count, n), 1)
    for i in range(chunks):
        span = pl.ds(i * count, count)
        a, b = own[span, :], other[span, :]
        left, right = jnp.where(even, a, b), jnp.where(even, b, a)
        panel = mmt(jnp.concatenate([left, right], axis=1), inverse)
        update = mm3(panel, mirrored)
        grow = (i * (count // n) + local // n) * ROWS + row
        rid = grow * n + local % n
        loads[i].wait()
        for j in range(4):
            cid = (j * COLS + col) * n + lane
            rows = pl.ds(j, count, stride=4)
            kept = data[i, rows, :] - update[:, j * n : (j + 1) * n]
            data[i, rows, :] = jnp.where(rid >= cid, kept, 0.0)

        @pl.when(col < 2)
        def _():
            solved = jnp.where(col == 0, panel[:, :n], panel[:, n:])
            if i == 0:
                first = jnp.where(col == 0, l11[...], 0.0)
                second = jnp.where(col == 0, l21[...], l22[...])
                solved = jnp.where(grow == 0, jnp.tile(first, (count // n, 1)), solved)
                solved = jnp.where(grow == 1, jnp.tile(second, (count // n, 1)), solved)
            data[i, pl.ds(0, count, stride=4), :] = jnp.where(rid >= col * n + lane, solved, 0.0)

        saves[i].start()
    for save in saves:
        save.wait()


def update(row, col, inverse, l11, l21, l22, own, other, here, there, view):
    vmem = pl.BlockSpec(memory_space=pltpu.VMEM)
    smem = pl.BlockSpec(memory_space=pltpu.SMEM)
    anywhere = pl.BlockSpec(memory_space=pl.ANY)
    return pl.pallas_call(
        update_kernel,
        in_specs=[smem] * 2 + [vmem] * 11 + [anywhere],
        out_specs=anywhere,
        out_shape=jax.ShapeDtypeStruct(view.shape, jnp.float32),
        scratch_shapes=[
            pltpu.VMEM((CHUNKS, view.shape[0] // CHUNKS, NB), jnp.float32),
            pltpu.SemaphoreType.DMA((CHUNKS,)),
            pltpu.SemaphoreType.DMA((CHUNKS,)),
        ],
        name="update",
    )(row, col, *inverse, l11, l21, l22, own, other, here, there, view)


def z_pairs(root, held, stride):
    pairs = []
    for layer in held:
        for core, sign in ((0, 1), (1, -1)):
            a = (root + sign * layer) % LAYERS
            b = (root + sign * (layer + stride)) % LAYERS
            if root == 0 or b > 0:
                pairs.append((2 * a + core, 2 * b + core))
    return pairs


def plane_pairs(first, second):
    pairs = []
    for core, rows in ((0, first), (1, second)):
        for z in range(LAYERS):
            pairs += [(a * COLS + 2 * z + core, b * COLS + 2 * z + core) for a, b in rows]
    return pairs


def shards(matrix):
    row = lax.axis_index("row")
    col = lax.axis_index("col")
    at_row, at_col = row.reshape(1), col.reshape(1)
    core, z = col % 2, col // 2
    layer = jnp.where(core == 0, z, (LAYERS - z) % LAYERS)
    after = jnp.where(core == 0, (z + LAYERS - 1) % LAYERS, (LAYERS + 1 - z) % LAYERS)
    x, y = row % SIDE, row // SIDE
    view = matrix.reshape(-1, NB)

    def tie(*values):
        return lax.optimization_barrier(values)

    def send(value, pairs):
        return lax.ppermute(value, "col", pairs)

    def send_plane(value, first, second):
        return lax.ppermute(value, ("row", "col"), plane_pairs(first, second))

    def choose(step, held, parts):
        kept = jnp.where(step == 2, parts[0], held)
        return jnp.where(step == 1, parts[1], jnp.where(step == 3, parts[2], kept))

    across = lambda ys: [(SIDE * q + a, SIDE * q + b) for q in ys for a, b in ((0, 3), (1, 2))]
    along = lambda ys, by, xs: [(SIDE * q + i, SIDE * (q + by) + i) for q in ys for i in xs]
    strip, view = tie(view[: 4 * NB], view)
    moved = send_plane(strip, across([0]), along([0], 2, (0, 1)))
    column = view.reshape(-1, 4, NB)[:, 0, :]
    sent = send(column, [(0, 2), (1, 3)])
    strip = jnp.where(jnp.where(core == 0, x >= 2, y == 2), moved, strip)
    moved = send_plane(strip, along([0], 2, range(4)), along([0, 2], 1, (0, 1)))
    strip = jnp.where(jnp.where(core == 0, y == 2, y % 2 == 1), moved, strip)
    moved = send_plane(strip, along([0, 2], 1, range(4)), across(range(4)))
    _, sent, column = tie(strip, sent, column)
    panel, column = column, sent
    sent = send(column, z_pairs(1, [0], 4))
    strip = jnp.where(jnp.where(core == 0, y % 2 == 1, x >= 2), moved, strip)
    swap = [(i, i ^ 1) for i in range(ROWS)]
    mine = strip[::4]
    theirs = send_plane(mine, swap, swap)
    _, sent, column = tie(strip, sent, column)
    column = jnp.where(after == 4, sent, column)
    sent = send(column, z_pairs(1, [0], 12) + z_pairs(1, [4], 4))
    column = jnp.where((after == 8) | (after == 12), sent, column)
    sent = send(column, z_pairs(1, range(0, 16, 4), 2))

    strip, theirs = tie(strip, theirs)
    facing = send_plane(strip, swap, swap)
    top = is_top(row)
    corner = jnp.stack([jnp.where(top, mine, theirs), jnp.where(top, theirs, mine)])
    other = send(corner, [(0, 1), (1, 0)])
    _, sent, column = tie(other, sent, column)
    column = jnp.where(after % 4 == 2, sent, column)
    sent = send(column, z_pairs(1, range(0, 16, 2), 1))
    corner, other, column = tie(corner, other, column)
    inv, l11, l21, l22 = factorise(at_col, corner, other)
    inv, facing = tie(inv, facing)

    parts = [send(inv, z_pairs(0, [0], 4 * q)) for q in (2, 1, 3)]
    *parts, column = tie(*parts, column)
    inv = choose(layer // 4, inv, parts)
    _, sent, column = tie(inv, sent, column)
    parts = [send(inv, z_pairs(0, [0, 4, 8, 12], q)) for q in (2, 1, 3)]
    *parts, sent, column = tie(*parts, sent, column)
    column = jnp.where(z == 0, panel, jnp.where(after % 2 == 1, sent, column))
    column_other = send(column, [(c, c ^ 1) for c in range(COLS)])
    *parts, column = tie(*parts, column)
    out = update(at_row, at_col, [inv, *parts], l11, l21, l22, column, column_other, strip, facing, view)
    return out.reshape(matrix.shape)


def solution(mesh):
    spec = P("row", None, None, "col", None, None)
    return jax.shard_map(shards, mesh=mesh, in_specs=(spec,), out_specs=spec, check_vma=False)
```

```python
import jax
import jax.numpy as jnp
from jax import lax
from jax.experimental import pallas as pl
from jax.experimental.pallas import tpu as pltpu
from jax.sharding import PartitionSpec as P

HIGHEST = lax.Precision.HIGHEST
ROWS = 16
COLS = 32
LAYERS = 16
SIDE = 4
NB = 128
HALF = 64
PIECE = 8
CHUNKS = 2


def mm(a, b):
    return lax.dot_general(
        a, b, (((1,), (0,)), ((), ())), precision=HIGHEST, preferred_element_type=jnp.float32
    )


def mmt(a, b):
    return lax.dot_general(
        a, b, (((1,), (1,)), ((), ())), precision=HIGHEST, preferred_element_type=jnp.float32
    )


def split(a):
    high = a.astype(jnp.bfloat16)
    return high, (a - high.astype(jnp.float32)).astype(jnp.bfloat16)


def mm3(a, b):
    ah, al = split(a)
    bh, bl = b
    dot = lambda x, y: lax.dot_general(x, y, (((1,), (0,)), ((), ())), preferred_element_type=jnp.float32)
    return dot(ah, bh) + (dot(ah, bl) + dot(al, bh))


def eliminate(block, work):
    n = HALF
    shape = (8, 2 * n)
    lane = lax.broadcasted_iota(jnp.int32, shape, 1)
    sub = lax.broadcasted_iota(jnp.int32, shape, 0)
    work[:, :n] = block
    parts = []
    for i in range(n // 8):
        unit = jnp.where(lane == n + 8 * i + sub, 1.0, 0.0)
        parts.append(jnp.where(lane < n, work[8 * i : 8 * i + 8, :], unit))
    out = []
    for a in range(n // 8):
        rest = range(a + 1, n // 8)
        cols = []
        for j in range(8):
            k = 8 * a + j
            cols.append(
                {i: jnp.broadcast_to(parts[i][:, k : k + 1], shape) for i in range(a, n // 8)}
            )
        e = [
            [jnp.broadcast_to(cols[j][a][i : i + 1, :], shape) for j in range(i + 1)]
            for i in range(8)
        ]
        rows = [jnp.broadcast_to(parts[a][k : k + 1, :], shape) for k in range(8)]
        strip = None
        for k in range(8):
            inv = 1.0 / e[k][k]
            for i in range(k + 1, 8):
                low = e[i][k] * inv
                for j in range(k + 1, i + 1):
                    e[i][j] = e[i][j] - low * e[j][k]
                rows[i] = rows[i] - low * rows[k]
            root = lax.rsqrt(e[k][k])
            root = root * (1.5 - 0.5 * e[k][k] * root * root)
            done = rows[k] * root
            strip = done if k == 0 else jnp.where(sub == k, done, strip)
            for i in rest:
                m = cols[k][i] * inv
                for j in range(k + 1, 8):
                    cols[j][i] = cols[j][i] - m * e[j][k]
                parts[i] = parts[i] - m * rows[k]
        out.append(strip)
    full = jnp.concatenate(out, axis=0)
    r = lax.broadcasted_iota(jnp.int32, (n, n), 0)
    c = lax.broadcasted_iota(jnp.int32, (n, n), 1)
    return jnp.where(r <= c, full[:, :n], 0.0), jnp.where(r >= c, full[:, n:], 0.0)


def factor_block(s, work, upper):
    h = HALF
    u11, i11 = eliminate(s[:h, :h], work)
    l21 = mmt(s[h:, :h], i11)
    t21 = mm(l21, i11)
    u22, i22 = eliminate(s[h:, h:] - mmt(l21, l21), work)
    upper[:h, :h] = u11
    upper[:h, h:] = l21.T
    upper[h:, :h] = jnp.zeros((h, h), jnp.float32)
    upper[h:, h:] = u22
    return i11, -mm(i22, t21), i22


def factor_kernel(col, own, other, packed, l11, l21, l22, work, upper, inv, blocks, sems):
    h, n = HALF, NB
    even = col[0] == 0

    def put(to, parts):
        to[:h, :h] = parts[0]
        to[:h, h:] = jnp.zeros((h, h), jnp.float32)
        to[h:, :h] = parts[1]
        to[h:, h:] = parts[2]

    @pl.when(col[0] < 2)
    def _():
        for i, (first, second, half) in enumerate(((own, other, 0), (own, other, 1), (other, own, 1))):

            @pl.when(even)
            def _():
                pltpu.make_async_copy(first.at[half], blocks.at[i], sems.at[i]).start()

            @pl.when(jnp.logical_not(even))
            def _():
                pltpu.make_async_copy(second.at[half], blocks.at[i], sems.at[i]).start()

        for i in range(3):
            pltpu.make_async_copy(own.at[0], blocks.at[i], sems.at[i]).wait()
        put(inv.at[0], factor_block(blocks[0], work, upper))
        l11[...] = upper[...].T
        i11 = inv[0]
        p = mmt(blocks[1], i11)
        t = mm(p, i11)
        l21[...] = p
        put(inv.at[1], factor_block(blocks[2] - mmt(p, p), work, upper))
        l22[...] = upper[...].T
        i22 = inv[1]
        r = lax.broadcasted_iota(jnp.int32, (n, n), 0)
        c = lax.broadcasted_iota(jnp.int32, (n, n), 1)
        packed[:n] = jnp.where(r >= c, i11, i22.T)
        packed[n : 2 * n] = -mm(i22, t)
        diagonal = jnp.sum(jnp.where(r == c, i22, 0.0), axis=0, keepdims=True)
        packed[2 * n :] = jnp.broadcast_to(diagonal, (8, n))


def factorise(col, own, other):
    block = jax.ShapeDtypeStruct((NB, NB), jnp.float32)
    vmem = pl.BlockSpec(memory_space=pltpu.VMEM)
    return pl.pallas_call(
        factor_kernel,
        in_specs=[pl.BlockSpec(memory_space=pltpu.SMEM)] + [pl.BlockSpec(memory_space=pl.ANY)] * 2,
        out_specs=[vmem] * 4,
        out_shape=[jax.ShapeDtypeStruct((2 * NB + 8, NB), jnp.float32), block, block, block],
        scratch_shapes=[
            pltpu.VMEM((HALF, NB), jnp.float32),
            pltpu.VMEM((NB, NB), jnp.float32),
            pltpu.VMEM((2, NB, NB), jnp.float32),
            pltpu.VMEM((3, NB, NB), jnp.float32),
            pltpu.SemaphoreType.DMA((3,)),
        ],
        name="factorise",
    )(col, own, other)


def is_top(row):
    x = row % SIDE
    return (x == 0) | (x == SIDE - 1)


def update_kernel(at_row, at_col, held, two, one, three, l11, l21, l22, own, other, here, there, store, out, *scratch):
    data, columns, strips, packed, corners, loads, saves, sems = scratch
    n = NB
    chunks, rows_of = data.shape[:2]
    row, col = at_row[0], at_col[0]
    core, z = col % 2, col // 2
    step = jnp.where(core == 0, z, LAYERS - z) % 4
    even, top = core == 0, is_top(row)

    def start(condition, source, target, sem):
        @pl.when(condition)
        def _():
            pltpu.make_async_copy(source, target, sem).start()

    for i, part in enumerate((held, one, two, three)):
        start(step == i, part, packed, sems.at[0])
    for i, (near, far) in enumerate(((here, there), (there, here))):
        start(top, near, strips.at[i], sems.at[1 + i])
        start(jnp.logical_not(top), far, strips.at[i], sems.at[1 + i])
    for i, (near, far) in enumerate(((own, other), (other, own))):
        start(even, near, columns.at[i], sems.at[3 + i])
        start(jnp.logical_not(even), far, columns.at[i], sems.at[3 + i])
    fetch = [
        pltpu.make_async_copy(store.at[pl.ds(i * rows_of, rows_of)], data.at[i], loads.at[i])
        for i in range(chunks)
    ]
    save = [
        pltpu.make_async_copy(data.at[i], out.at[pl.ds(i * rows_of, rows_of)], saves.at[i])
        for i in range(chunks)
    ]
    for copy in fetch:
        copy.start()
    final = [pltpu.make_async_copy(l, corners.at[i], sems.at[5 + i]) for i, l in enumerate((l11, l21, l22))]

    @pl.when(col < 2)
    def _():
        for copy in final:
            copy.start()

    pltpu.make_async_copy(held, packed, sems.at[0]).wait()
    r = lax.broadcasted_iota(jnp.int32, (n, n), 0)
    c = lax.broadcasted_iota(jnp.int32, (n, n), 1)
    shared = packed[:n]
    i11 = jnp.where(r >= c, shared, 0.0)
    diagonal = jnp.where(r == c, packed[2 * n : 2 * n + 1], 0.0)
    i22 = jnp.where(r > c, shared.T, diagonal)
    inverse = jnp.concatenate(
        [
            jnp.concatenate([i11, jnp.zeros((n, n), jnp.float32)], axis=1),
            jnp.concatenate([packed[n : 2 * n], i22], axis=1),
        ],
        axis=0,
    )
    halves = []
    for i in range(2):
        pltpu.make_async_copy(here, strips.at[i], sems.at[1 + i]).wait()
        halves.append(jnp.concatenate([strips[i, pl.ds(j, n, stride=4), :] for j in range(4)], axis=1))
    mirrored = split(mm(inverse, jnp.concatenate(halves, axis=0)))
    for i in range(2):
        pltpu.make_async_copy(own, columns.at[i], sems.at[3 + i]).wait()
    count = rows_of // 4
    local = lax.broadcasted_iota(jnp.int32, (count, n), 0)
    lane = lax.broadcasted_iota(jnp.int32, (count, n), 1)
    for i in range(chunks):
        span = pl.ds(i * count, count)
        panel = mmt(jnp.concatenate([columns[0, span, :], columns[1, span, :]], axis=1), inverse)
        update = mm3(panel, mirrored)
        grow = (i * (count // n) + local // n) * ROWS + row
        rid = grow * n + local % n
        fetch[i].wait()
        for j in range(4):
            cid = (j * COLS + col) * n + lane
            rows = pl.ds(j, count, stride=4)
            kept = data[i, rows, :] - update[:, j * n : (j + 1) * n]
            data[i, rows, :] = jnp.where(rid >= cid, kept, 0.0)

        @pl.when(col < 2)
        def _():
            solved = jnp.where(col == 0, panel[:, :n], panel[:, n:])
            if i == 0:
                for copy in final:
                    copy.wait()
                first = jnp.where(col == 0, corners[0], 0.0)
                second = jnp.where(col == 0, corners[1], corners[2])
                solved = jnp.where(grow == 0, jnp.tile(first, (count // n, 1)), solved)
                solved = jnp.where(grow == 1, jnp.tile(second, (count // n, 1)), solved)
            data[i, pl.ds(0, count, stride=4), :] = jnp.where(rid >= col * n + lane, solved, 0.0)

        save[i].start()
    for copy in save:
        copy.wait()


def update(row, col, inverse, l11, l21, l22, own, other, here, there, view):
    smem = pl.BlockSpec(memory_space=pltpu.SMEM)
    anywhere = pl.BlockSpec(memory_space=pl.ANY)
    return pl.pallas_call(
        update_kernel,
        in_specs=[smem] * 2 + [anywhere] * 12,
        out_specs=anywhere,
        out_shape=jax.ShapeDtypeStruct(view.shape, jnp.float32),
        scratch_shapes=[
            pltpu.VMEM((CHUNKS, view.shape[0] // CHUNKS, NB), jnp.float32),
            pltpu.VMEM((2, *own.shape), jnp.float32),
            pltpu.VMEM((2, *here.shape), jnp.float32),
            pltpu.VMEM(inverse[0].shape, jnp.float32),
            pltpu.VMEM((3, NB, NB), jnp.float32),
            pltpu.SemaphoreType.DMA((CHUNKS,)),
            pltpu.SemaphoreType.DMA((CHUNKS,)),
            pltpu.SemaphoreType.DMA((8,)),
        ],
        name="update",
    )(row, col, *inverse, l11, l21, l22, own, other, here, there, view)


def z_pairs(root, held, stride):
    pairs = []
    for layer in held:
        for core, sign in ((0, 1), (1, -1)):
            a = (root + sign * layer) % LAYERS
            b = (root + sign * (layer + stride)) % LAYERS
            if root == 0 or b > 0:
                pairs.append((2 * a + core, 2 * b + core))
    return pairs


def plane_pairs(first, second):
    pairs = []
    for core, rows in ((0, first), (1, second)):
        for z in range(LAYERS):
            pairs += [(a * COLS + 2 * z + core, b * COLS + 2 * z + core) for a, b in rows]
    return pairs


def shards(matrix):
    row = lax.axis_index("row")
    col = lax.axis_index("col")
    at_row, at_col = row.reshape(1), col.reshape(1)
    core, z = col % 2, col // 2
    layer = jnp.where(core == 0, z, (LAYERS - z) % LAYERS)
    after = jnp.where(core == 0, (z + LAYERS - 1) % LAYERS, (LAYERS + 1 - z) % LAYERS)
    x, y = row % SIDE, row // SIDE
    view = matrix.reshape(-1, NB)

    def tie(*values):
        return lax.optimization_barrier(values)

    def send(value, pairs):
        return lax.ppermute(value, "col", pairs)

    def send_plane(value, first, second):
        return lax.ppermute(value, ("row", "col"), plane_pairs(first, second))

    def choose(step, held, parts):
        kept = jnp.where(step == 2, parts[0], held)
        return jnp.where(step == 1, parts[1], jnp.where(step == 3, parts[2], kept))

    across = lambda ys: [(SIDE * q + a, SIDE * q + b) for q in ys for a, b in ((0, 3), (1, 2))]
    along = lambda ys, by, xs: [(SIDE * q + i, SIDE * (q + by) + i) for q in ys for i in xs]
    strip, view = tie(view[: 4 * NB], view)
    moved = send_plane(strip, across([0]), along([0], 2, (0, 1)))
    column = view.reshape(-1, 4, NB)[:, 0, :]
    sent = send(column, [(0, 2), (1, 3)])
    strip = jnp.where(jnp.where(core == 0, x >= 2, y == 2), moved, strip)
    moved = send_plane(strip, along([0], 2, range(4)), along([0, 2], 1, (0, 1)))
    strip = jnp.where(jnp.where(core == 0, y == 2, y % 2 == 1), moved, strip)
    moved = send_plane(strip, along([0, 2], 1, range(4)), across(range(4)))
    _, sent, column = tie(strip, sent, column)
    panel, column = column, sent
    sent = send(column, z_pairs(1, [0], 4))
    strip = jnp.where(jnp.where(core == 0, y % 2 == 1, x >= 2), moved, strip)
    swap = [(i, i ^ 1) for i in range(ROWS)]
    mine = strip[::4]
    theirs = send_plane(mine, swap, swap)
    _, sent, column = tie(strip, sent, column)
    column = jnp.where(after == 4, sent, column)
    sent = send(column, z_pairs(1, [0], 12) + z_pairs(1, [4], 4))
    column = jnp.where((after == 8) | (after == 12), sent, column)
    sent = send(column, z_pairs(1, range(0, 16, 4), 2))

    strip, theirs = tie(strip, theirs)
    facing = send_plane(strip, swap, swap)
    top = is_top(row)
    corner = jnp.stack([jnp.where(top, mine, theirs), jnp.where(top, theirs, mine)])
    other = send(corner, [(0, 1), (1, 0)])
    _, sent, column = tie(other, sent, column)
    column = jnp.where(after % 4 == 2, sent, column)
    sent = send(column, z_pairs(1, range(0, 16, 2), 1))
    corner, other, column = tie(corner, other, column)
    inv, l11, l21, l22 = factorise(at_col, corner, other)
    inv, facing = tie(inv, facing)

    parts = [send(inv, z_pairs(0, [0], 4 * q)) for q in (2, 1, 3)]
    *parts, column = tie(*parts, column)
    inv = choose(layer // 4, inv, parts)
    _, sent, column = tie(inv, sent, column)
    parts = [send(inv, z_pairs(0, [0, 4, 8, 12], q)) for q in (2, 1, 3)]
    *parts, sent, column = tie(*parts, sent, column)
    column = jnp.where(z == 0, panel, jnp.where(after % 2 == 1, sent, column))
    column_other = send(column, [(c, c ^ 1) for c in range(COLS)])
    *parts, column = tie(*parts, column)
    out = update(at_row, at_col, [inv, *parts], l11, l21, l22, column, column_other, strip, facing, view)
    return out.reshape(matrix.shape)


def solution(mesh):
    spec = P("row", None, None, "col", None, None)
    return jax.shard_map(shards, mesh=mesh, in_specs=(spec,), out_specs=spec, check_vma=False)
```
